512 devices in a mesh: pts: 512 (over y, x, z, core).
Axes of the slice: x: 4, y: 4, z: 16, core: 2. Of those that a mesh axis runs over, the one named last changes fastest.
Arguments:
- points: bfloat16 [64, 1048576], P(None, 'pts'), may hold values from -6 to 6
- inv_scale: float32 [64], replicated, may hold values from 0.05 to 0.25
- vectors: bfloat16 [32, 1048576], P(None, 'pts'), may hold values from -0.59765625 to 0.59765625
Outputs:
- product: float32 [32, 1048576], P(None, 'pts')
The draws below stay inside these ranges and needn't reach their ends.
All inputs are finite; a program needn't handle non-finite values.
Results may differ from the reference program's by a relative error of at most 0.0003.
Values sent between devices are 32-bit elements; how exact they have to be, the bound alone decides.
No kernel may reach another device: no remote copies, remote signals or barrier semaphores. Data moves between devices by JAX's collectives and lax.ppermute only.
A program may use at most 64 MiB of HBM per device.

```python
import math
import jax
import jax.numpy as jnp
from jax import lax

F = 64
V = 32
BLOCK = 2048
ROUNDS = 2
POINTS = 1048576
N_PTS = 512


def level_of(own_key, dims, split, low, top_value):
    factor_of, own = 1.0, jax.random.fold_in(own_key, 6)
    for axis_at, blocks in split:
        heights = jnp.exp(jax.random.uniform(jax.random.fold_in(own, axis_at), (blocks,), jnp.float32, low / len(split), top_value / len(split)))
        factor_of = factor_of * jnp.repeat(heights, dims[axis_at] // blocks).reshape([-1 if axis == axis_at else 1 for axis in range(len(dims))])
    return factor_of


def bell_draw(key, shape, deviation, most, shards=(), kind=jnp.bfloat16):
    level = level_of(key, shape, shards, -0.22, 0.18) if shards else 1.0
    values = jax.random.normal(key, shape, jnp.float32) * deviation * level
    return jnp.minimum(jnp.maximum(values, -most), most).astype(kind)


def setup_inputs(seed: int = 0) -> dict:
    key_of = jax.random.split(jax.random.key(seed), 4)
    points = bell_draw(key_of[0], (F, POINTS), 1.0, 6.0, ((1, 512),))
    inv_scale = jnp.clip(jnp.exp(jax.random.uniform(key_of[1], (F,), jnp.float32, math.log(0.05), math.log(0.25))), 0.05, 0.25)
    vectors = bell_draw(key_of[2], (V, POINTS), 0.1, 0.59765625, ((1, 512),))
    return {"points": points, "inv_scale": inv_scale, "vectors": vectors}


def kernel_tile(rows, cols):
    sq_rows = jnp.sum(rows * rows, axis=0)
    sq_cols = jnp.sum(cols * cols, axis=0)
    cross = lax.dot_general(rows, cols, (((0,), (0,)), ((), ())), precision=lax.Precision.HIGHEST, preferred_element_type=jnp.float32)
    dist = sq_rows[:, None] + sq_cols[None, :] - 2.0 * cross
    return jnp.exp(-0.5 * dist)


def reference(points, inv_scale, vectors):
    scaled = points.astype(jnp.float32) * inv_scale[:, None]
    blocks = N_PTS
    scaled_blocks = jnp.transpose(scaled.reshape(F, blocks, BLOCK), (1, 0, 2))
    vector_blocks = jnp.transpose(vectors.astype(jnp.float32).reshape(V, blocks, BLOCK), (1, 0, 2))

    def one_block(index):
        mine = scaled_blocks[index]
        own_vec = vector_blocks[index]
        kern = kernel_tile(mine, mine)
        total = lax.dot_general(own_vec, kern, (((1,), (1,)), ((), ())), precision=lax.Precision.HIGHEST, preferred_element_type=jnp.float32)
        for step in range(1, ROUNDS + 1):
            ahead = ((index + step) % blocks).astype(jnp.int32)
            behind = ((index - step + blocks) % blocks).astype(jnp.int32)
            kern_ahead = kernel_tile(mine, scaled_blocks[ahead])
            total = total + lax.dot_general(vector_blocks[ahead], kern_ahead, (((1,), (1,)), ((), ())), precision=lax.Precision.HIGHEST, preferred_element_type=jnp.float32)
            kern_behind = kernel_tile(scaled_blocks[behind], mine)
            total = total + lax.dot_general(vector_blocks[behind], kern_behind, (((1,), (0,)), ((), ())), precision=lax.Precision.HIGHEST, preferred_element_type=jnp.float32)
        return total

    result = lax.map(one_block, jnp.arange(blocks, dtype=jnp.int32))
    return jnp.transpose(result, (1, 0, 2)).reshape(V, blocks * BLOCK)
```

```python
import jax
import jax.numpy as jnp
from jax import lax
from jax.experimental import pallas as pl
from jax.experimental.pallas import tpu as pltpu
from jax.sharding import PartitionSpec as P

F32 = jnp.float32
BF16 = jnp.bfloat16
FEATS = 64
DEPTH = 256
SIDE = 256
GROUP = 4
LOG2E = 1.4426950408889634


def three(value):
    high = value.astype(BF16).astype(F32)
    rest = value - high
    mid = rest.astype(BF16).astype(F32)
    low = (rest - mid).astype(BF16).astype(F32)
    return high, mid, low


def extra_rows(rows):
    width = rows[0].shape[1]
    which = lax.broadcasted_iota(jnp.int32, (8, width), 0)
    top = jnp.zeros((8, width), F32)
    for at, row in enumerate(rows):
        top = jnp.where(which == at, row, top)
    return jnp.concatenate([top, jnp.zeros((FEATS - 8, width), F32)], axis=0)


def half_norms(part, scale):
    scaled = part * scale
    return jnp.sum(scaled * scaled, axis=0, keepdims=True) * (-0.5 * LOG2E)


def own_side(block_ref, scale_ref, right_ref):
    scale = scale_ref[...]
    squared = scale * scale * LOG2E

    def step(at, unused):
        columns = pl.ds(pl.multiple_of(at * SIDE, SIDE), SIDE)
        part = block_ref[0:FEATS, columns]
        one = jnp.ones((1, SIDE), F32)
        weighted = three(part * squared)
        extra = extra_rows(list(three(half_norms(part, scale))) + [one, one, one])
        right_ref[:, columns] = jnp.concatenate(list(weighted) + [extra], axis=0).astype(BF16)
        return unused

    lax.fori_loop(0, block_ref.shape[1] // SIDE, step, 0)


def other_side(block_ref, scale_ref, left_ref, vec_ref):
    scale = scale_ref[...]

    def step(at, unused):
        columns = pl.ds(pl.multiple_of(at * SIDE, SIDE), SIDE)
        part = block_ref[0:FEATS, columns]
        one = jnp.ones((1, SIDE), F32)
        extra = extra_rows([one, one, one] + list(three(half_norms(part, scale))))
        whole = jnp.concatenate([part, part, part, extra], axis=0)
        left_ref[columns, :] = jnp.transpose(whole).astype(BF16)
        return unused

    lax.fori_loop(0, block_ref.shape[1] // SIDE, step, 0)
    vec_ref[...] = block_ref[FEATS:, :].astype(BF16)


def add_tile(left_ref, right_ref, vec_ref, total_ref):
    count = right_ref.shape[1]
    span = GROUP * SIDE

    def step(at, unused):
        rows_at = pl.multiple_of((at % (count // span)) * span, span)
        cols_at = pl.multiple_of((at // (count // span)) * span, span)
        for across in range(GROUP):
            columns = pl.ds(pl.multiple_of(cols_at + across * SIDE, SIDE), SIDE)
            total = total_ref[:, columns]
            for down in range(GROUP):
                rows = pl.ds(pl.multiple_of(rows_at + down * SIDE, SIDE), SIDE)
                exponent = jnp.dot(
                    left_ref[rows, :], right_ref[:, columns], preferred_element_type=F32
                )
                kern = jnp.exp2(exponent)
                high = kern.astype(BF16)
                low = (kern - high.astype(F32)).astype(BF16)
                vec = vec_ref[:, rows]
                total = total + jnp.dot(vec, high, preferred_element_type=F32)
                total = total + jnp.dot(vec, low, preferred_element_type=F32)
            total_ref[:, columns] = total
        return unused

    lax.fori_loop(0, (count // span) ** 2, step, 0)


def first_kernel(block_ref, scale_ref, right_ref, total_ref, left_ref, vec_ref):
    own_side(block_ref, scale_ref, right_ref)
    other_side(block_ref, scale_ref, left_ref, vec_ref)
    total_ref[...] = jnp.zeros_like(total_ref)
    add_tile(left_ref, right_ref, vec_ref, total_ref)


def next_kernel(block_ref, scale_ref, right_ref, before_ref, total_ref, left_ref, vec_ref):
    other_side(block_ref, scale_ref, left_ref, vec_ref)
    total_ref[...] = before_ref[...]
    add_tile(left_ref, right_ref, vec_ref, total_ref)


def scratch(count, width):
    return [pltpu.VMEM((count, DEPTH), BF16), pltpu.VMEM((width, count), BF16)]


def params():
    return pltpu.CompilerParams(vmem_limit_bytes=24 << 20)


def cost(count, width):
    return pl.CostEstimate(
        flops=2 * count * count * (DEPTH + 8 * width),
        bytes_accessed=4 << 20,
        transcendentals=count * count,
    )


def first_tile(block, scale):
    count, width = block.shape[1], block.shape[0] - FEATS
    return pl.pallas_call(
        first_kernel,
        out_shape=(
            jax.ShapeDtypeStruct((DEPTH, count), BF16),
            jax.ShapeDtypeStruct((width, count), F32),
        ),
        scratch_shapes=scratch(count, width),
        compiler_params=params(),
        cost_estimate=cost(count, width),
        name="own_tile",
    )(block, scale)


def next_tile(block, scale, right, total):
    count, width = block.shape[1], block.shape[0] - FEATS
    return pl.pallas_call(
        next_kernel,
        out_shape=jax.ShapeDtypeStruct((width, count), F32),
        scratch_shapes=scratch(count, width),
        compiler_params=params(),
        cost_estimate=cost(count, width),
        name="other_tile",
    )(block, scale, right, total)


def per_device(points, inv_scale, vectors):
    count = lax.axis_size("pts")
    block = jnp.concatenate([points.astype(F32), vectors.astype(F32)], axis=0)
    scale = inv_scale[:, None]
    pair = [(at, at ^ 1) for at in range(count)]
    near = [(at, (at - 2 if at % 2 == 0 else at + 2) % count) for at in range(count)]
    far = [(at, (at + 2 if at % 2 == 0 else at - 2) % count) for at in range(count)]
    from_near = lax.ppermute(block, "pts", near)
    from_far = lax.ppermute(block, "pts", far)
    from_pair = lax.ppermute(block, "pts", pair)
    from_both = lax.ppermute(from_near, "pts", pair)
    right, total = first_tile(block, scale)
    for other in (from_pair, from_near, from_both, from_far):
        total = next_tile(other, scale, right, total)
    return total


def solution(mesh):
    return jax.shard_map(
        per_device,
        mesh=mesh,
        in_specs=(P(None, "pts"), P(), P(None, "pts")),
        out_specs=P(None, "pts"),
        check_vma=False,
    )
```

```python
import jax
import jax.numpy as jnp
from jax import lax
from jax.experimental import pallas as pl
from jax.experimental.pallas import tpu as pltpu
from jax.sharding import PartitionSpec as P

F32 = jnp.float32
BF16 = jnp.bfloat16
FEATS = 64
DEPTH = 256
SIDE = 256
DOWN = 4
RUN = 32
EARLY = 2
LOG2E = 1.4426950408889634


def three(value):
    high = value.astype(BF16).astype(F32)
    rest = value - high
    mid = rest.astype(BF16).astype(F32)
    low = (rest - mid).astype(BF16).astype(F32)
    return high, mid, low


def extra_rows(rows):
    width = rows[0].shape[1]
    which = lax.broadcasted_iota(jnp.int32, (8, width), 0)
    top = jnp.zeros((8, width), F32)
    for at, row in enumerate(rows):
        top = jnp.where(which == at, row, top)
    return jnp.concatenate([top, jnp.zeros((FEATS - 8, width), F32)], axis=0)


def weigh(part, squared):
    value = part * squared
    high = value.astype(BF16).astype(F32)
    mid = (value - high).astype(BF16).astype(F32)
    norm = jnp.sum(part * (high + mid), axis=0, keepdims=True) * -0.5
    return high, mid, norm


def own_side(block_ref, scale_ref, right_ref):
    squared = scale_ref[...] * scale_ref[...] * LOG2E

    def step(at, unused):
        columns = pl.ds(pl.multiple_of(at * SIDE, SIDE), SIDE)
        high, mid, norm = weigh(block_ref[0:FEATS, columns], squared)
        one = jnp.ones((1, SIDE), F32)
        extra = extra_rows(list(three(norm)) + [one, one, one])
        zero = jnp.zeros((FEATS, SIDE), F32)
        right_ref[:, columns] = jnp.concatenate([high, extra, mid, zero], axis=0).astype(BF16)
        return unused

    lax.fori_loop(0, block_ref.shape[1] // SIDE, step, 0)


def other_side(block_ref, scale_ref, left_ref, vec_ref):
    squared = scale_ref[...] * scale_ref[...] * LOG2E

    def step(at, unused):
        columns = pl.ds(pl.multiple_of(at * SIDE, SIDE), SIDE)
        part = block_ref[0:FEATS, columns]
        high, mid, norm = weigh(part, squared)
        one = jnp.ones((1, SIDE), F32)
        extra = extra_rows([one, one, one] + list(three(norm)))
        left_ref[columns, :] = jnp.transpose(jnp.concatenate([part, extra], axis=0)).astype(BF16)
        return unused

    lax.fori_loop(0, block_ref.shape[1] // SIDE, step, 0, unroll=2)
    vec_ref[...] = block_ref[FEATS:, :].astype(BF16)


def add_tile(left_ref, right_ref, vec_ref, total_ref):
    count = right_ref.shape[1]
    span = DOWN * SIDE

    def step(at, unused):
        for across in range(count // SIDE):
            columns = slice(across * SIDE, (across + 1) * SIDE)
            total = total_ref[:, columns]
            for down in range(DOWN):
                rows = pl.ds(pl.multiple_of(at * span + down * SIDE, SIDE), SIDE)
                left = left_ref[rows, :]
                exponent = jnp.dot(
                    jnp.concatenate([left, left], axis=1),
                    right_ref[:, columns],
                    preferred_element_type=F32,
                )
                kern = jnp.exp2(exponent)
                high = kern.astype(BF16)
                low = (kern - high.astype(F32)).astype(BF16)
                vec = vec_ref[:, rows]
                total = total + jnp.dot(vec, high, preferred_element_type=F32)
                total = total + jnp.dot(vec, low, preferred_element_type=F32)
            total_ref[:, columns] = total
        return unused

    lax.fori_loop(0, count // span, step, 0)


def own_tile(block_ref, scale_ref, right_ref, total_ref, left_ref, vec_ref):
    own_side(block_ref, scale_ref, right_ref)
    other_side(block_ref, scale_ref, left_ref, vec_ref)
    total_ref[...] = jnp.zeros_like(total_ref)
    add_tile(left_ref, right_ref, vec_ref, total_ref)


def before_kernel(
    flag_ref, points_ref, vectors_ref, scale_ref, block_ref, right_ref, total_ref, left_ref, vec_ref
):
    block_ref[0:FEATS, :] = points_ref[...].astype(F32)
    block_ref[FEATS:, :] = vectors_ref[...].astype(F32)

    @pl.when(flag_ref[0] == 1)
    def _():
        own_tile(block_ref, scale_ref, right_ref, total_ref, left_ref, vec_ref)


def after_kernel(
    flag_ref, block_ref, scale_ref, right_in, total_in, right_ref, total_ref, left_ref, vec_ref
):
    @pl.when(flag_ref[0] == 0)
    def _():
        own_tile(block_ref, scale_ref, right_ref, total_ref, left_ref, vec_ref)

    @pl.when(flag_ref[0] == 1)
    def _():
        right_ref[...] = right_in[...]
        total_ref[...] = total_in[...]


def next_kernel(block_ref, scale_ref, right_ref, before_ref, total_ref, left_ref, vec_ref):
    other_side(block_ref, scale_ref, left_ref, vec_ref)
    total_ref[...] = before_ref[...]
    add_tile(left_ref, right_ref, vec_ref, total_ref)


def call(body, name, outs, count, width, flops, scalars=0, inputs=0):
    specs = [pl.BlockSpec(memory_space=pltpu.SMEM)] * scalars
    specs += [pl.BlockSpec(memory_space=pltpu.VMEM)] * inputs
    return pl.pallas_call(
        body,
        in_specs=specs,
        out_shape=outs,
        scratch_shapes=[pltpu.VMEM((count, DEPTH // 2), BF16), pltpu.VMEM((width, count), BF16)],
        compiler_params=pltpu.CompilerParams(vmem_limit_bytes=24 << 20),
        cost_estimate=pl.CostEstimate(
            flops=flops, bytes_accessed=4 << 20, transcendentals=count * count
        ),
        name=name,
    )


def per_device(points, inv_scale, vectors):
    devices = lax.axis_size("pts")
    count, width = points.shape[1], vectors.shape[0]
    scale = inv_scale[:, None]
    work = 2 * count * count * (DEPTH + 8 * width)
    whole = jax.ShapeDtypeStruct((FEATS + width, count), F32)
    right_type = jax.ShapeDtypeStruct((DEPTH, count), BF16)
    total_type = jax.ShapeDtypeStruct((width, count), F32)
    flag = (lax.axis_index("pts") % RUN < EARLY).astype(jnp.int32).reshape(1)
    block, right, total = call(
        before_kernel, "own_before", (whole, right_type, total_type), count, width, 0, 1, 3
    )(flag, points, vectors, scale)
    pair = [(at, at ^ 1) for at in range(devices)]
    near = [(at, (at - 2 if at % 2 == 0 else at + 2) % devices) for at in range(devices)]
    far = [(at, (at + 2 if at % 2 == 0 else at - 2) % devices) for at in range(devices)]
    from_near = lax.ppermute(block, "pts", near)
    from_far = lax.ppermute(block, "pts", far)
    from_pair = lax.ppermute(block, "pts", pair)
    from_both = lax.ppermute(from_near, "pts", pair)
    right, total = call(
        after_kernel, "own_after", (right_type, total_type), count, width, work, 1, 4
    )(flag, block, scale, right, total)
    for other in (from_pair, from_near, from_both, from_far):
        total = call(next_kernel, "other_tile", total_type, count, width, work, 0, 4)(
            other, scale, right, total
        )
    return total


def solution(mesh):
    return jax.shard_map(
        per_device,
        mesh=mesh,
        in_specs=(P(None, "pts"), P(), P(None, "pts")),
        out_specs=P(None, "pts"),
        check_vma=False,
    )
```

```python
import jax
import jax.numpy as jnp
from jax import lax
from jax.experimental import pallas as pl
from jax.experimental.pallas import tpu as pltpu
from jax.sharding import PartitionSpec as P

F32 = jnp.float32
BF16 = jnp.bfloat16
FEATS = 64
DEPTH = 256
SIDE = 256
DOWN = 4
RUN = 32
EARLY = 2
LOG2E = 1.4426950408889634


def three(value):
    high = value.astype(BF16).astype(F32)
    rest = value - high
    mid = rest.astype(BF16).astype(F32)
    low = (rest - mid).astype(BF16).astype(F32)
    return high, mid, low


def extra_rows(rows):
    width = rows[0].shape[1]
    which = lax.broadcasted_iota(jnp.int32, (8, width), 0)
    top = jnp.zeros((8, width), F32)
    for at, row in enumerate(rows):
        top = jnp.where(which == at, row, top)
    return jnp.concatenate([top, jnp.zeros((FEATS - 8, width), F32)], axis=0)


def weigh(part, squared):
    value = part * squared
    high = value.astype(BF16).astype(F32)
    mid = (value - high).astype(BF16).astype(F32)
    norm = jnp.sum(part * (high + mid), axis=0, keepdims=True) * -0.5
    return high, mid, norm


def own_side(block_ref, scale_ref, right_ref):
    squared = scale_ref[...] * scale_ref[...] * LOG2E

    def step(at, unused):
        columns = pl.ds(pl.multiple_of(at * SIDE, SIDE), SIDE)
        high, mid, norm = weigh(block_ref[0:FEATS, columns], squared)
        one = jnp.ones((1, SIDE), F32)
        extra = extra_rows(list(three(norm)) + [one, one, one])
        zero = jnp.zeros((FEATS, SIDE), F32)
        right_ref[:, columns] = jnp.concatenate([high, extra, mid, zero], axis=0).astype(BF16)
        return unused

    lax.fori_loop(0, block_ref.shape[1] // SIDE, step, 0)


def other_side(block_ref, scale_ref, left_ref, vec_ref):
    squared = scale_ref[...] * scale_ref[...] * LOG2E

    def step(at, unused):
        columns = pl.ds(pl.multiple_of(at * SIDE, SIDE), SIDE)
        part = block_ref[0:FEATS, columns]
        high, mid, norm = weigh(part, squared)
        one = jnp.ones((1, SIDE), F32)
        extra = extra_rows([one, one, one] + list(three(norm)))
        left_ref[columns, :] = jnp.transpose(jnp.concatenate([part, extra], axis=0)).astype(BF16)
        return unused

    lax.fori_loop(0, block_ref.shape[1] // SIDE, step, 0, unroll=2)
    vec_ref[...] = block_ref[FEATS:, :].astype(BF16)


def add_tile(left_ref, right_ref, vec_ref, total_ref):
    count = right_ref.shape[1]
    span = DOWN * SIDE

    def step(at, unused):
        for across in range(count // SIDE):
            columns = slice(across * SIDE, (across + 1) * SIDE)
            total = total_ref[:, columns]
            for down in range(DOWN):
                rows = pl.ds(pl.multiple_of(at * span + down * SIDE, SIDE), SIDE)
                left = left_ref[rows, :]
                exponent = jnp.dot(
                    jnp.concatenate([left, left], axis=1),
                    right_ref[:, columns],
                    preferred_element_type=F32,
                )
                kern = jnp.exp2(exponent)
                high = kern.astype(BF16)
                low = (kern - high.astype(F32)).astype(BF16)
                vec = vec_ref[:, rows]
                total = total + jnp.dot(vec, high, preferred_element_type=F32)
                total = total + jnp.dot(vec, low, preferred_element_type=F32)
            total_ref[:, columns] = total
        return unused

    lax.fori_loop(0, count // span, step, 0)


def own_tile(block_ref, scale_ref, right_ref, total_ref, left_ref, vec_ref):
    own_side(block_ref, scale_ref, right_ref)
    other_side(block_ref, scale_ref, left_ref, vec_ref)
    total_ref[...] = jnp.zeros_like(total_ref)
    add_tile(left_ref, right_ref, vec_ref, total_ref)


def before_kernel(
    flag_ref, block_ref, scale_ref, again_ref, right_ref, total_ref, left_ref, vec_ref
):
    again_ref[...] = block_ref[...]

    @pl.when(flag_ref[0] == 1)
    def _():
        own_tile(block_ref, scale_ref, right_ref, total_ref, left_ref, vec_ref)


def after_kernel(
    flag_ref, block_ref, scale_ref, right_in, total_in, right_ref, total_ref, left_ref, vec_ref
):
    @pl.when(flag_ref[0] == 0)
    def _():
        own_tile(block_ref, scale_ref, right_ref, total_ref, left_ref, vec_ref)

    @pl.when(flag_ref[0] == 1)
    def _():
        right_ref[...] = right_in[...]
        total_ref[...] = total_in[...]


def next_kernel(block_ref, scale_ref, right_ref, before_ref, total_ref, left_ref, vec_ref):
    other_side(block_ref, scale_ref, left_ref, vec_ref)
    total_ref[...] = before_ref[...]
    add_tile(left_ref, right_ref, vec_ref, total_ref)


def call(body, name, outs, count, width, flops, scalars=0, inputs=0):
    specs = [pl.BlockSpec(memory_space=pltpu.SMEM)] * scalars
    specs += [pl.BlockSpec(memory_space=pltpu.VMEM)] * inputs
    return pl.pallas_call(
        body,
        in_specs=specs,
        out_shape=outs,
        scratch_shapes=[pltpu.VMEM((count, DEPTH // 2), BF16), pltpu.VMEM((width, count), BF16)],
        compiler_params=pltpu.CompilerParams(vmem_limit_bytes=24 << 20),
        cost_estimate=pl.CostEstimate(
            flops=flops, bytes_accessed=4 << 20, transcendentals=count * count
        ),
        name=name,
    )


def per_device(points, inv_scale, vectors):
    devices = lax.axis_size("pts")
    count, width = points.shape[1], vectors.shape[0]
    scale = inv_scale[:, None]
    work = 2 * count * count * (DEPTH + 8 * width)
    whole = jax.ShapeDtypeStruct((FEATS + width, count), F32)
    right_type = jax.ShapeDtypeStruct((DEPTH, count), BF16)
    total_type = jax.ShapeDtypeStruct((width, count), F32)
    flag = (lax.axis_index("pts") % RUN < EARLY).astype(jnp.int32).reshape(1)
    pair = [(at, at ^ 1) for at in range(devices)]
    near = [(at, (at - 2 if at % 2 == 0 else at + 2) % devices) for at in range(devices)]
    far = [(at, (at + 2 if at % 2 == 0 else at - 2) % devices) for at in range(devices)]
    block = jnp.concatenate([points.astype(F32), vectors.astype(F32)], axis=0)
    from_pair = lax.ppermute(block, "pts", pair)
    again, right, total = call(
        before_kernel, "own_before", (whole, right_type, total_type), count, width, 0, 1, 2
    )(flag, block, scale)
    from_near = lax.ppermute(again, "pts", near)
    from_far = lax.ppermute(again, "pts", far)
    right, total = call(
        after_kernel, "own_after", (right_type, total_type), count, width, work, 1, 4
    )(flag, again, scale, right, total)

    def add(other, total):
        return call(next_kernel, "other_tile", total_type, count, width, work, 0, 4)(
            other, scale, right, total
        )

    total = add(from_pair, total)
    from_near, total = lax.optimization_barrier((from_near, total))
    from_both = lax.ppermute(from_near, "pts", pair)
    for other in (from_near, from_both, from_far):
        total = add(other, total)
    return total


def solution(mesh):
    return jax.shard_map(
        per_device,
        mesh=mesh,
        in_specs=(P(None, "pts"), P(), P(None, "pts")),
        out_specs=P(None, "pts"),
        check_vma=False,
    )
```

```python
import jax
import jax.numpy as jnp
from jax import lax
from jax.experimental import pallas as pl
from jax.experimental.pallas import tpu as pltpu
from jax.sharding import PartitionSpec as P

F32 = jnp.float32
BF16 = jnp.bfloat16
FEATS = 64
DEPTH = 256
SIDE = 256
DOWN = 4
RUN = 32
EARLY = 2
WORK = 32
LOG2E = 1.4426950408889634


def three(value):
    high = value.astype(BF16).astype(F32)
    rest = value - high
    mid = rest.astype(BF16).astype(F32)
    low = (rest - mid).astype(BF16).astype(F32)
    return high, mid, low


def extra_rows(rows):
    width = rows[0].shape[1]
    which = lax.broadcasted_iota(jnp.int32, (8, width), 0)
    top = jnp.zeros((8, width), F32)
    for at, row in enumerate(rows):
        top = jnp.where(which == at, row, top)
    return jnp.concatenate([top, jnp.zeros((FEATS - 8, width), F32)], axis=0)


def weigh(part, squared):
    value = part * squared
    high = value.astype(BF16).astype(F32)
    mid = (value - high).astype(BF16).astype(F32)
    norm = jnp.sum(part * (high + mid), axis=0, keepdims=True) * -0.5
    return high, mid, norm


def own_side(block_ref, scale_ref, right_ref):
    squared = scale_ref[...] * scale_ref[...] * LOG2E

    def step(at, unused):
        columns = pl.ds(pl.multiple_of(at * SIDE, SIDE), SIDE)
        high, mid, norm = weigh(block_ref[0:FEATS, columns], squared)
        one = jnp.ones((1, SIDE), F32)
        extra = extra_rows(list(three(norm)) + [one, one, one])
        zero = jnp.zeros((FEATS, SIDE), F32)
        right_ref[:, columns] = jnp.concatenate([high, extra, mid, zero], axis=0).astype(BF16)
        return unused

    lax.fori_loop(0, block_ref.shape[1] // SIDE, step, 0)


def other_side(block_ref, scale_ref, left_ref, vec_ref):
    squared = scale_ref[...] * scale_ref[...] * LOG2E

    def step(at, unused):
        columns = pl.ds(pl.multiple_of(at * SIDE, SIDE), SIDE)
        part = block_ref[0:FEATS, columns]
        high, mid, norm = weigh(part, squared)
        one = jnp.ones((1, SIDE), F32)
        extra = extra_rows([one, one, one] + list(three(norm)))
        left_ref[columns, :] = jnp.transpose(jnp.concatenate([part, extra], axis=0)).astype(BF16)
        return unused

    lax.fori_loop(0, block_ref.shape[1] // SIDE, step, 0, unroll=2)
    vec_ref[...] = block_ref[FEATS:, :].astype(BF16)


def add_tile(left_ref, right_ref, vec_ref, total_ref):
    count = right_ref.shape[1]
    span = DOWN * SIDE

    def step(at, unused):
        for across in range(count // SIDE):
            columns = slice(across * SIDE, (across + 1) * SIDE)
            total = total_ref[:, columns]
            for down in range(DOWN):
                rows = pl.ds(pl.multiple_of(at * span + down * SIDE, SIDE), SIDE)
                left = left_ref[rows, :]
                exponent = jnp.dot(
                    jnp.concatenate([left, left], axis=1),
                    right_ref[:, columns],
                    preferred_element_type=F32,
                )
                kern = jnp.exp2(exponent)
                high = kern.astype(BF16)
                low = (kern - high.astype(F32)).astype(BF16)
                vec = vec_ref[:, rows]
                total = total + jnp.dot(vec, high, preferred_element_type=F32)
                total = total + jnp.dot(vec, low, preferred_element_type=F32)
            total_ref[:, columns] = total
        return unused

    lax.fori_loop(0, count // span, step, 0)


def own_tile(block_ref, scale_ref, right_ref, total_ref, left_ref, vec_ref):
    own_side(block_ref, scale_ref, right_ref)
    other_side(block_ref, scale_ref, left_ref, vec_ref)
    total_ref[...] = jnp.zeros_like(total_ref)
    add_tile(left_ref, right_ref, vec_ref, total_ref)


def before_kernel(
    flag_ref, block_ref, scale_ref, again_ref, right_ref, total_ref, left_ref, vec_ref
):
    again_ref[...] = block_ref[...]

    @pl.when(flag_ref[0] == 1)
    def _():
        own_tile(block_ref, scale_ref, right_ref, total_ref, left_ref, vec_ref)


def after_kernel(
    flag_ref, block_ref, scale_ref, right_in, total_in, right_ref, total_ref, left_ref, vec_ref
):
    @pl.when(flag_ref[0] == 0)
    def _():
        own_tile(block_ref, scale_ref, right_ref, total_ref, left_ref, vec_ref)

    @pl.when(flag_ref[0] == 1)
    def _():
        right_ref[...] = right_in[...]
        total_ref[...] = total_in[...]


def next_kernel(block_ref, scale_ref, right_ref, before_ref, total_ref, left_ref, vec_ref):
    other_side(block_ref, scale_ref, left_ref, vec_ref)
    total_ref[...] = before_ref[...]
    add_tile(left_ref, right_ref, vec_ref, total_ref)


def call(body, name, outs, count, width, flops, scalars=0, inputs=0):
    specs = [pl.BlockSpec(memory_space=pltpu.SMEM)] * scalars
    specs += [pl.BlockSpec(memory_space=pltpu.VMEM)] * inputs
    return pl.pallas_call(
        body,
        in_specs=specs,
        out_shape=outs,
        scratch_shapes=[pltpu.VMEM((count, DEPTH // 2), BF16), pltpu.VMEM((width, count), BF16)],
        compiler_params=pltpu.CompilerParams(vmem_limit_bytes=24 << 20),
        cost_estimate=pl.CostEstimate(
            flops=flops, bytes_accessed=1 << 20, transcendentals=0
        ),
        name=name,
    )


def per_device(points, inv_scale, vectors):
    devices = lax.axis_size("pts")
    count, width = points.shape[1], vectors.shape[0]
    scale = inv_scale[:, None]
    work = count * count * WORK
    whole = jax.ShapeDtypeStruct((FEATS + width, count), F32)
    right_type = jax.ShapeDtypeStruct((DEPTH, count), BF16)
    total_type = jax.ShapeDtypeStruct((width, count), F32)
    index = lax.axis_index("pts")
    flag = ((index % RUN < EARLY) & (index > 0)).astype(jnp.int32).reshape(1)
    pair = [(at, at ^ 1) for at in range(devices)]
    near = [(at, (at - 2 if at % 2 == 0 else at + 2) % devices) for at in range(devices)]
    far = [(at, (at + 2 if at % 2 == 0 else at - 2) % devices) for at in range(devices)]
    block = jnp.concatenate([points.astype(F32), vectors.astype(F32)], axis=0)
    again, right, total = call(
        before_kernel, "own_before", (whole, right_type, total_type), count, width, 0, 1, 2
    )(flag, block, scale)
    from_pair = lax.ppermute(again, "pts", pair)
    from_near = lax.ppermute(again, "pts", near)
    from_far = lax.ppermute(again, "pts", far)
    right, total = call(
        after_kernel, "own_after", (right_type, total_type), count, width, work, 1, 4
    )(flag, again, scale, right, total)

    def add(other, total):
        return call(next_kernel, "other_tile", total_type, count, width, work, 0, 4)(
            other, scale, right, total
        )

    total = add(from_pair, total)
    from_near, total = lax.optimization_barrier((from_near, total))
    from_both = lax.ppermute(from_near, "pts", pair)
    total = add(from_near, total)
    from_far, total = lax.optimization_barrier((from_far, total))
    total = add(from_far, total)
    total = add(from_both, total)
    return total


def solution(mesh):
    return jax.shard_map(
        per_device,
        mesh=mesh,
        in_specs=(P(None, "pts"), P(), P(None, "pts")),
        out_specs=P(None, "pts"),
        check_vma=False,
    )
```

```python
import jax
import jax.numpy as jnp
from jax import lax
from jax.experimental import pallas as pl
from jax.experimental.pallas import tpu as pltpu
from jax.sharding import PartitionSpec as P

F32 = jnp.float32
BF16 = jnp.bfloat16
FEATS = 64
DEPTH = 256
SIDE = 256
DOWN = 8
RUN = 32
EARLY = 2
WORK = 32
LOG2E = 1.4426950408889634


def three(value):
    high = value.astype(BF16).astype(F32)
    rest = value - high
    mid = rest.astype(BF16).astype(F32)
    low = (rest - mid).astype(BF16).astype(F32)
    return high, mid, low


def extra_rows(rows):
    width = rows[0].shape[1]
    which = lax.broadcasted_iota(jnp.int32, (8, width), 0)
    top = jnp.zeros((8, width), F32)
    for at, row in enumerate(rows):
        top = jnp.where(which == at, row, top)
    return jnp.concatenate([top, jnp.zeros((FEATS - 8, width), F32)], axis=0)


def weigh(part, squared):
    value = part * squared
    high = value.astype(BF16).astype(F32)
    mid = (value - high).astype(BF16).astype(F32)
    norm = jnp.sum(part * (high + mid), axis=0, keepdims=True) * -0.5
    return high, mid, norm


def own_side(block_ref, scale_ref, right_ref):
    squared = scale_ref[...] * scale_ref[...] * LOG2E

    def step(at, unused):
        columns = pl.ds(pl.multiple_of(at * SIDE, SIDE), SIDE)
        high, mid, norm = weigh(block_ref[0:FEATS, columns], squared)
        one = jnp.ones((1, SIDE), F32)
        extra = extra_rows(list(three(norm)) + [one, one, one])
        zero = jnp.zeros((FEATS, SIDE), F32)
        right_ref[:, columns] = jnp.concatenate([high, extra, mid, zero], axis=0).astype(BF16)
        return unused

    lax.fori_loop(0, block_ref.shape[1] // SIDE, step, 0)


def other_side(block_ref, scale_ref, left_ref, vec_ref):
    squared = scale_ref[...] * scale_ref[...] * LOG2E

    def step(at, unused):
        columns = slice(at * SIDE, (at + 1) * SIDE)
        part = block_ref[0:FEATS, columns]
        high, mid, norm = weigh(part, squared)
        one = jnp.ones((1, SIDE), F32)
        extra = extra_rows([one, one, one] + list(three(norm)))
        left_ref[columns, :] = jnp.transpose(jnp.concatenate([part, extra], axis=0)).astype(BF16)
        return unused

    for at in range(block_ref.shape[1] // SIDE):
        step(at, 0)
    vec_ref[...] = block_ref[FEATS:, :].astype(BF16)


def add_tile(left_ref, right_ref, vec_ref, total_ref):
    count = right_ref.shape[1]
    span = DOWN * SIDE

    def step(at, unused):
        for across in range(count // SIDE):
            columns = slice(across * SIDE, (across + 1) * SIDE)
            total = total_ref[:, columns]
            for down in range(DOWN):
                rows = slice(at * span + down * SIDE, at * span + (down + 1) * SIDE)
                left = left_ref[rows, :]
                exponent = jnp.dot(
                    jnp.concatenate([left, left], axis=1),
                    right_ref[:, columns],
                    preferred_element_type=F32,
                )
                kern = jnp.exp2(exponent)
                high = kern.astype(BF16)
                low = (kern - high.astype(F32)).astype(BF16)
                vec = vec_ref[:, rows]
                total = total + jnp.dot(vec, high, preferred_element_type=F32)
                total = total + jnp.dot(vec, low, preferred_element_type=F32)
            total_ref[:, columns] = total
        return unused

    for at in range(count // span):
        step(at, 0)


def own_tile(block_ref, scale_ref, right_ref, total_ref, left_ref, vec_ref):
    own_side(block_ref, scale_ref, right_ref)
    other_side(block_ref, scale_ref, left_ref, vec_ref)
    total_ref[...] = jnp.zeros_like(total_ref)
    add_tile(left_ref, right_ref, vec_ref, total_ref)


def before_kernel(
    flag_ref, block_ref, scale_ref, again_ref, right_ref, total_ref, left_ref, vec_ref
):
    again_ref[...] = block_ref[...]

    @pl.when(flag_ref[0] == 1)
    def _():
        own_tile(block_ref, scale_ref, right_ref, total_ref, left_ref, vec_ref)


def after_kernel(
    flag_ref, block_ref, scale_ref, right_in, total_in, right_ref, total_ref, left_ref, vec_ref
):
    @pl.when(flag_ref[0] == 0)
    def _():
        own_tile(block_ref, scale_ref, right_ref, total_ref, left_ref, vec_ref)

    @pl.when(flag_ref[0] == 1)
    def _():
        right_ref[...] = right_in[...]
        total_ref[...] = total_in[...]


def next_kernel(block_ref, scale_ref, right_ref, before_ref, total_ref, left_ref, vec_ref):
    other_side(block_ref, scale_ref, left_ref, vec_ref)
    total_ref[...] = before_ref[...]
    add_tile(left_ref, right_ref, vec_ref, total_ref)


def call(body, name, outs, count, width, flops, scalars=0, inputs=0):
    specs = [pl.BlockSpec(memory_space=pltpu.SMEM)] * scalars
    specs += [pl.BlockSpec(memory_space=pltpu.VMEM)] * inputs
    return pl.pallas_call(
        body,
        in_specs=specs,
        out_shape=outs,
        scratch_shapes=[pltpu.VMEM((count, DEPTH // 2), BF16), pltpu.VMEM((width, count), BF16)],
        compiler_params=pltpu.CompilerParams(vmem_limit_bytes=24 << 20),
        cost_estimate=pl.CostEstimate(
            flops=flops, bytes_accessed=1 << 20, transcendentals=0
        ),
        name=name,
    )


def per_device(points, inv_scale, vectors):
    devices = lax.axis_size("pts")
    count, width = points.shape[1], vectors.shape[0]
    scale = inv_scale[:, None]
    work = count * count * WORK
    whole = jax.ShapeDtypeStruct((FEATS + width, count), F32)
    right_type = jax.ShapeDtypeStruct((DEPTH, count), BF16)
    total_type = jax.ShapeDtypeStruct((width, count), F32)
    index = lax.axis_index("pts")
    flag = ((index % RUN < EARLY) & (index > 0)).astype(jnp.int32).reshape(1)
    pair = [(at, at ^ 1) for at in range(devices)]
    near = [(at, (at - 2 if at % 2 == 0 else at + 2) % devices) for at in range(devices)]
    far = [(at, (at + 2 if at % 2 == 0 else at - 2) % devices) for at in range(devices)]
    block = jnp.concatenate([points.astype(F32), vectors.astype(F32)], axis=0)
    again, right, total = call(
        before_kernel, "own_before", (whole, right_type, total_type), count, width, 0, 1, 2
    )(flag, block, scale)
    from_pair = lax.ppermute(again, "pts", pair)
    from_near = lax.ppermute(again, "pts", near)
    from_far = lax.ppermute(again, "pts", far)
    right, total = call(
        after_kernel, "own_after", (right_type, total_type), count, width, work, 1, 4
    )(flag, again, scale, right, total)

    def add(other, total):
        return call(next_kernel, "other_tile", total_type, count, width, work, 0, 4)(
            other, scale, right, total
        )

    total = add(from_pair, total)
    from_near, total = lax.optimization_barrier((from_near, total))
    from_both = lax.ppermute(from_near, "pts", pair)
    total = add(from_near, total)
    from_far, total = lax.optimization_barrier((from_far, total))
    total = add(from_far, total)
    total = add(from_both, total)
    return total


def solution(mesh):
    return jax.shard_map(
        per_device,
        mesh=mesh,
        in_specs=(P(None, "pts"), P(), P(None, "pts")),
        out_specs=P(None, "pts"),
        check_vma=False,
    )
```

```python
import jax
import jax.numpy as jnp
from jax import lax
from jax.experimental import pallas as pl
from jax.experimental.pallas import tpu as pltpu
from jax.sharding import PartitionSpec as P

F32 = jnp.float32
BF16 = jnp.bfloat16
FEATS = 64
DEPTH = 256
SIDE = 256
DOWN = 8
RUN = 32
EARLY = 2
WORK = 32
LOG2E = 1.4426950408889634


def three(value):
    high = value.astype(BF16).astype(F32)
    rest = value - high
    mid = rest.astype(BF16).astype(F32)
    low = (rest - mid).astype(BF16).astype(F32)
    return high, mid, low


def extra_rows(rows):
    width = rows[0].shape[1]
    which = lax.broadcasted_iota(jnp.int32, (8, width), 0)
    top = jnp.zeros((8, width), F32)
    for at, row in enumerate(rows):
        top = jnp.where(which == at, row, top)
    return jnp.concatenate([top, jnp.zeros((FEATS - 8, width), F32)], axis=0)


def weigh(part, squared):
    value = part * squared
    high = value.astype(BF16).astype(F32)
    mid = (value - high).astype(BF16).astype(F32)
    norm = jnp.sum(part * (high + mid), axis=0, keepdims=True) * -0.5
    return high, mid, norm


def own_side(block_ref, scale_ref, right_ref):
    squared = scale_ref[...] * scale_ref[...] * LOG2E

    def step(at, unused):
        columns = pl.ds(pl.multiple_of(at * SIDE, SIDE), SIDE)
        high, mid, norm = weigh(block_ref[0:FEATS, columns], squared)
        one = jnp.ones((1, SIDE), F32)
        extra = extra_rows(list(three(norm)) + [one, one, one])
        zero = jnp.zeros((FEATS, SIDE), F32)
        right_ref[:, columns] = jnp.concatenate([high, extra, mid, zero], axis=0).astype(BF16)
        return unused

    lax.fori_loop(0, block_ref.shape[1] // SIDE, step, 0)


def other_side(block_ref, scale_ref, left_ref, vec_ref):
    squared = scale_ref[...] * scale_ref[...] * LOG2E

    def step(at, unused):
        columns = slice(at * SIDE, (at + 1) * SIDE)
        part = block_ref[0:FEATS, columns]
        high, mid, norm = weigh(part, squared)
        one = jnp.ones((1, SIDE), F32)
        extra = extra_rows([one, one, one] + list(three(norm)))
        left_ref[columns, :] = jnp.transpose(jnp.concatenate([part, extra], axis=0)).astype(BF16)
        return unused

    for at in range(block_ref.shape[1] // SIDE):
        step(at, 0)
    vec_ref[...] = block_ref[FEATS:, :].astype(BF16)


def add_tile(left_ref, right_ref, vec_ref, total_ref):
    count = right_ref.shape[1]
    span = DOWN * SIDE

    def step(at, unused):
        for across in range(count // SIDE):
            columns = slice(across * SIDE, (across + 1) * SIDE)
            total = total_ref[:, columns]
            for down in range(DOWN):
                rows = slice(at * span + down * SIDE, at * span + (down + 1) * SIDE)
                left = left_ref[rows, :]
                exponent = jnp.dot(
                    jnp.concatenate([left, left], axis=1),
                    right_ref[:, columns],
                    preferred_element_type=F32,
                )
                kern = jnp.exp2(exponent)
                high = kern.astype(BF16)
                low = (kern - high.astype(F32)).astype(BF16)
                vec = vec_ref[:, rows]
                total = total + jnp.dot(vec, high, preferred_element_type=F32)
                total = total + jnp.dot(vec, low, preferred_element_type=F32)
            total_ref[:, columns] = total
        return unused

    for at in range(count // span):
        step(at, 0)


def before_kernel(
    flag_ref, block_ref, scale_ref, again_ref, right_ref, total_ref, left_ref, vec_ref
):
    again_ref[...] = block_ref[...]
    own_side(block_ref, scale_ref, right_ref)
    total_ref[...] = jnp.zeros_like(total_ref)

    @pl.when(flag_ref[0] == 1)
    def _():
        other_side(block_ref, scale_ref, left_ref, vec_ref)
        add_tile(left_ref, right_ref, vec_ref, total_ref)


def after_kernel(
    flag_ref, block_ref, scale_ref, right_ref, before_ref, total_ref, left_ref, vec_ref
):
    total_ref[...] = before_ref[...]

    @pl.when(flag_ref[0] == 0)
    def _():
        other_side(block_ref, scale_ref, left_ref, vec_ref)
        add_tile(left_ref, right_ref, vec_ref, total_ref)


def next_kernel(block_ref, scale_ref, right_ref, before_ref, total_ref, left_ref, vec_ref):
    other_side(block_ref, scale_ref, left_ref, vec_ref)
    total_ref[...] = before_ref[...]
    add_tile(left_ref, right_ref, vec_ref, total_ref)


def call(body, name, outs, count, width, flops, scalars=0, inputs=0):
    specs = [pl.BlockSpec(memory_space=pltpu.SMEM)] * scalars
    specs += [pl.BlockSpec(memory_space=pltpu.VMEM)] * inputs
    return pl.pallas_call(
        body,
        in_specs=specs,
        out_shape=outs,
        scratch_shapes=[pltpu.VMEM((count, DEPTH // 2), BF16), pltpu.VMEM((width, count), BF16)],
        compiler_params=pltpu.CompilerParams(vmem_limit_bytes=24 << 20),
        cost_estimate=pl.CostEstimate(
            flops=flops, bytes_accessed=1 << 20, transcendentals=0
        ),
        name=name,
    )


def per_device(points, inv_scale, vectors):
    devices = lax.axis_size("pts")
    count, width = points.shape[1], vectors.shape[0]
    scale = inv_scale[:, None]
    work = count * count * WORK
    whole = jax.ShapeDtypeStruct((FEATS + width, count), F32)
    right_type = jax.ShapeDtypeStruct((DEPTH, count), BF16)
    total_type = jax.ShapeDtypeStruct((width, count), F32)
    index = lax.axis_index("pts")
    flag = ((index % RUN < EARLY) & (index > 0)).astype(jnp.int32).reshape(1)
    pair = [(at, at ^ 1) for at in range(devices)]
    near = [(at, (at - 2 if at % 2 == 0 else at + 2) % devices) for at in range(devices)]
    far = [(at, (at + 2 if at % 2 == 0 else at - 2) % devices) for at in range(devices)]
    block = jnp.concatenate([points.astype(F32), vectors.astype(F32)], axis=0)
    again, right, total = call(
        before_kernel, "own_before", (whole, right_type, total_type), count, width, 0, 1, 2
    )(flag, block, scale)
    from_pair = lax.ppermute(again, "pts", pair)
    from_near = lax.ppermute(again, "pts", near)

    def add(other, total):
        return call(next_kernel, "other_tile", total_type, count, width, work, 0, 4)(
            other, scale, right, total
        )

    total = add(from_pair, total)
    later, total = lax.optimization_barrier((again, total))
    from_far = lax.ppermute(later, "pts", far)
    total = call(after_kernel, "own_after", total_type, count, width, work, 1, 4)(
        flag, again, scale, right, total
    )
    from_near, total = lax.optimization_barrier((from_near, total))
    from_both = lax.ppermute(from_near, "pts", pair)
    total = add(from_near, total)
    from_far, total = lax.optimization_barrier((from_far, total))
    total = add(from_far, total)
    total = add(from_both, total)
    return total


def solution(mesh):
    return jax.shard_map(
        per_device,
        mesh=mesh,
        in_specs=(P(None, "pts"), P(), P(None, "pts")),
        out_specs=P(None, "pts"),
        check_vma=False,
    )
```

```python
import jax
import jax.numpy as jnp
from jax import lax
from jax.experimental import pallas as pl
from jax.experimental.pallas import tpu as pltpu
from jax.sharding import PartitionSpec as P

F32 = jnp.float32
BF16 = jnp.bfloat16
FEATS = 64
DEPTH = 256
SIDE = 256
DOWN = 8
RUN = 32
EARLY = 2
WORK = 32
LOG2E = 1.4426950408889634


def three(value):
    high = value.astype(BF16).astype(F32)
    rest = value - high
    mid = rest.astype(BF16).astype(F32)
    low = (rest - mid).astype(BF16).astype(F32)
    return high, mid, low


def extra_rows(rows):
    width = rows[0].shape[1]
    which = lax.broadcasted_iota(jnp.int32, (8, width), 0)
    top = jnp.zeros((8, width), F32)
    for at, row in enumerate(rows):
        top = jnp.where(which == at, row, top)
    return jnp.concatenate([top, jnp.zeros((FEATS - 8, width), F32)], axis=0)


def weigh(part, squared):
    value = part * squared
    high = value.astype(BF16).astype(F32)
    mid = (value - high).astype(BF16).astype(F32)
    norm = jnp.sum(part * (high + mid), axis=0, keepdims=True) * -0.5
    return high, mid, norm


def own_side(block_ref, scale_ref, right_ref):
    squared = scale_ref[...] * scale_ref[...] * LOG2E

    def step(at, unused):
        columns = pl.ds(pl.multiple_of(at * SIDE, SIDE), SIDE)
        high, mid, norm = weigh(block_ref[0:FEATS, columns], squared)
        one = jnp.ones((1, SIDE), F32)
        extra = extra_rows(list(three(norm)) + [one, one, one])
        zero = jnp.zeros((FEATS, SIDE), F32)
        right_ref[:, columns] = jnp.concatenate([high, extra, mid, zero], axis=0).astype(BF16)
        return unused

    lax.fori_loop(0, block_ref.shape[1] // SIDE, step, 0)


def other_side(block_ref, scale_ref, left_ref, vec_ref):
    squared = scale_ref[...] * scale_ref[...] * LOG2E

    def step(at, unused):
        columns = slice(at * SIDE, (at + 1) * SIDE)
        part = block_ref[0:FEATS, columns]
        high, mid, norm = weigh(part, squared)
        one = jnp.ones((1, SIDE), F32)
        extra = extra_rows([one, one, one] + list(three(norm)))
        left_ref[columns, :] = jnp.transpose(jnp.concatenate([part, extra], axis=0)).astype(BF16)
        return unused

    for at in range(block_ref.shape[1] // SIDE):
        step(at, 0)
    vec_ref[...] = block_ref[FEATS:, :].astype(BF16)


def add_tile(left_ref, right_ref, vec_ref, total_ref):
    count = right_ref.shape[1]
    span = DOWN * SIDE

    def step(at, unused):
        for across in range(count // SIDE):
            columns = slice(across * SIDE, (across + 1) * SIDE)
            total = total_ref[:, columns]
            for down in range(DOWN):
                rows = slice(at * span + down * SIDE, at * span + (down + 1) * SIDE)
                left = left_ref[rows, :]
                exponent = jnp.dot(
                    jnp.concatenate([left, left], axis=1),
                    right_ref[:, columns],
                    preferred_element_type=F32,
                )
                kern = jnp.exp2(exponent)
                high = kern.astype(BF16)
                low = (kern - high.astype(F32)).astype(BF16)
                vec = vec_ref[:, rows]
                total = total + jnp.dot(vec, high, preferred_element_type=F32)
                total = total + jnp.dot(vec, low, preferred_element_type=F32)
            total_ref[:, columns] = total
        return unused

    for at in range(count // span):
        step(at, 0)


def before_kernel(
    flag_ref, block_ref, scale_ref, again_ref, right_ref, total_ref, left_ref, vec_ref
):
    again_ref[...] = block_ref[...]
    own_side(block_ref, scale_ref, right_ref)
    total_ref[...] = jnp.zeros_like(total_ref)

    @pl.when(flag_ref[0] == 1)
    def _():
        other_side(block_ref, scale_ref, left_ref, vec_ref)
        add_tile(left_ref, right_ref, vec_ref, total_ref)


def after_kernel(
    flag_ref, block_ref, scale_ref, right_ref, before_ref, total_ref, left_ref, vec_ref
):
    total_ref[...] = before_ref[...]

    @pl.when(flag_ref[0] == 0)
    def _():
        other_side(block_ref, scale_ref, left_ref, vec_ref)
        add_tile(left_ref, right_ref, vec_ref, total_ref)


def next_kernel(block_ref, scale_ref, right_ref, before_ref, total_ref, left_ref, vec_ref):
    other_side(block_ref, scale_ref, left_ref, vec_ref)
    total_ref[...] = before_ref[...]
    add_tile(left_ref, right_ref, vec_ref, total_ref)


def call(body, name, outs, count, width, flops, scalars=0, inputs=0):
    specs = [pl.BlockSpec(memory_space=pltpu.SMEM)] * scalars
    specs += [pl.BlockSpec(memory_space=pltpu.VMEM)] * inputs
    return pl.pallas_call(
        body,
        in_specs=specs,
        out_shape=outs,
        scratch_shapes=[pltpu.VMEM((count, DEPTH // 2), BF16), pltpu.VMEM((width, count), BF16)],
        compiler_params=pltpu.CompilerParams(vmem_limit_bytes=24 << 20),
        cost_estimate=pl.CostEstimate(
            flops=flops, bytes_accessed=1 << 20, transcendentals=0
        ),
        name=name,
    )


def per_device(points, inv_scale, vectors):
    devices = lax.axis_size("pts")
    count, width = points.shape[1], vectors.shape[0]
    scale = inv_scale[:, None]
    work = count * count * WORK
    whole = jax.ShapeDtypeStruct((FEATS + width, count), F32)
    right_type = jax.ShapeDtypeStruct((DEPTH, count), BF16)
    total_type = jax.ShapeDtypeStruct((width, count), F32)
    index = lax.axis_index("pts")
    flag = ((index % RUN < EARLY)).astype(jnp.int32).reshape(1)
    pair = [(at, at ^ 1) for at in range(devices)]
    near = [(at, (at - 2 if at % 2 == 0 else at + 2) % devices) for at in range(devices)]
    far = [(at, (at + 2 if at % 2 == 0 else at - 2) % devices) for at in range(devices)]
    block = jnp.concatenate([points.astype(F32), vectors.astype(F32)], axis=0)
    again, right, total = call(
        before_kernel, "own_before", (whole, right_type, total_type), count, width, 0, 1, 2
    )(flag, block, scale)
    from_pair = lax.ppermute(again, "pts", pair)
    from_near = lax.ppermute(again, "pts", near)

    def add(other, total):
        return call(next_kernel, "other_tile", total_type, count, width, work, 0, 4)(
            other, scale, right, total
        )

    total = add(from_pair, total)
    later, total = lax.optimization_barrier((again, total))
    from_far = lax.ppermute(later, "pts", far)
    total = call(after_kernel, "own_after", total_type, count, width, work, 1, 4)(
        flag, again, scale, right, total
    )
    from_near, total = lax.optimization_barrier((from_near, total))
    from_both = lax.ppermute(from_near, "pts", pair)
    total = add(from_near, total)
    from_far, total = lax.optimization_barrier((from_far, total))
    total = add(from_far, total)
    total = add(from_both, total)
    return total


def solution(mesh):
    return jax.shard_map(
        per_device,
        mesh=mesh,
        in_specs=(P(None, "pts"), P(), P(None, "pts")),
        out_specs=P(None, "pts"),
        check_vma=False,
    )
```
